32 devices in a mesh: groups: 2 (over y), band: 4 (over z), wave: 2 (over x), probe: 2 (over core).
Axes of the slice: x: 2, y: 2, z: 4, core: 2. Of those that a mesh axis runs over, the one named last changes fastest.
Arguments:
- probes_spec: bfloat16 [8, 8, 2, 640, 1280], P(('groups', 'probe'), None, None, ('band', 'wave')), parts along dimension 0, may hold values from -6 to 6
- legendre: bfloat16 [640, 16, 1280], P(('band', 'wave')), may hold values from -0.15625 to 0.15625
- wave_order: int32 [640], replicated, may hold values from 0 to 639, each once
- obs_weight: float32 [4, 4096], P(None, ('groups', 'band', 'wave')), parts along dimension 1, may hold values from 0.25 to 4
- send_rows: int32 [16, 8, 32], P(('groups', 'band', 'wave')), parts along dimension 0, may hold values from 0 to 255, as said below
- send_counts: int32 [16, 8], P('groups'), parts along dimension 0, may hold values from 8 to 32, as said below
- interp_idx: int32 [4, 16, 8, 32], P(None, ('groups', 'band', 'wave')), parts along dimension 1, may hold values from 0 to 5119, as said below
- interp_weight: float32 [4, 16, 8, 32], P(None, ('groups', 'band', 'wave')), parts along dimension 1, may hold values from 0 to 1, as said below
Outputs:
- product: bfloat16 [8, 8, 2, 640, 1280], P(('groups', 'probe'), None, None, ('band', 'wave')), parts along dimension 0
The draws below stay inside these ranges and needn't reach their ends.
There are 2 independent parts, one for each index of `groups`. The reference program is written for one: setup_inputs(seed, part) draws one part's arguments, and reference() takes and returns one part's arrays. A program takes and returns all parts, laid end to end along the dimension named above; an argument that names none is the same for every part. Nothing has to cross between parts.
Inputs may be any that keep to these rules, and one draw needn't show every extreme that they name: For each source r, the entries of send_rows[r] are a permutation of 0 to 255. `send_counts`: a count of live slots, at least 8; in every draw one band owner receives 32 live slots from every source. `interp_idx`: the four entries of a slot are the points (i, j), (i, j + 1 mod 1280), (i + 1, j), (i + 1, j + 1 mod 1280) of the band owner's rows, as i * 1280 + j. `interp_weight`: the four weights of a slot are nonnegative and sum to 1.
All inputs are finite; a program needn't handle non-finite values.
Results may differ from the reference program's by a relative error of at most 0.0083.
Values may be sent and summed in bfloat16 or wider, within the bound.
A program may use at most 64 MiB of HBM per device.

```python
import math
import jax
import jax.numpy as jnp
from jax import lax

NN = 1280
MW = 640
NLON = 1280
LF = 8
PROBES = 4
LAT_DEV = 4
CAP = 32
BANDS = 4
WAVES = 2
NODES = 8
LAT = 16
LFD = 4
OBS_DEV = 256
OBS = 2048


def draw_send_counts(key, part):
    key_dense, key_hot, key_mult = jax.random.split(key, 3)
    density = jax.random.randint(key_dense, (BANDS,), 2, 5)
    hot_node = jax.random.randint(key_hot, (), 0, NODES)
    band_ids = jnp.arange(BANDS)
    density = jnp.where(band_ids == hot_node // WAVES, 4, density)
    multiple = jax.random.randint(key_mult, (NODES, NODES), CAP // 8, CAP // 4 + 1)
    dest_band = jnp.arange(NODES) // WAVES
    counts = jnp.minimum(CAP, density[dest_band][None, :] * multiple)
    counts = jnp.where(jnp.arange(NODES)[None, :] == hot_node, CAP, counts)
    return counts.astype(jnp.int32)


def draw_send_rows(key, part):
    source_keys = jax.random.split(key, NODES)
    orderings = jax.vmap(lambda one_key: jax.random.permutation(one_key, NODES * CAP))(source_keys)
    return orderings.reshape(NODES, NODES, CAP).astype(jnp.int32)


def draw_interp_idx(key, part):
    key_lat, key_lon = jax.random.split(key, 2)
    rows_lat = jax.random.randint(key_lat, (NODES, NODES, CAP), 0, LAT_DEV - 1)
    cols_lon = jax.random.randint(key_lon, (NODES, NODES, CAP), 0, NLON)
    rows_lat = rows_lat.at[:, 0, 0].set(LAT_DEV - 2).at[:, 0, 1].set(0)
    cols_lon = cols_lon.at[:, 0, 0].set(NLON - 2).at[:, 0, 1].set(0)
    eastern = (cols_lon + 1) % NLON
    corners = jnp.stack([rows_lat * NLON + cols_lon, rows_lat * NLON + eastern, (rows_lat + 1) * NLON + cols_lon, (rows_lat + 1) * NLON + eastern])
    return corners.astype(jnp.int32)


def draw_interp_weight(key, part):
    key_north, key_east = jax.random.split(key, 2)
    northward = jax.random.uniform(key_north, (NODES, NODES, CAP), jnp.float32)
    eastward = jax.random.uniform(key_east, (NODES, NODES, CAP), jnp.float32)
    weights = jnp.stack([(1.0 - northward) * (1.0 - eastward), (1.0 - northward) * eastward, northward * (1.0 - eastward), northward * eastward])
    return weights.astype(jnp.float32)


def block_levels(own_key, shape, cuts, low, high):
    factor_of = 1.0
    for dim, parts in cuts:
        steps = jax.random.uniform(jax.random.fold_in(jax.random.fold_in(own_key, 6), dim), (parts,), jnp.float32, low / len(cuts), high / len(cuts))
        factor_of = factor_of * jnp.repeat(jnp.exp(steps), shape[dim] // parts).reshape((-1,) + (1,) * (len(shape) - 1 - dim))
    return factor_of


def bell_draw(stream_key, extent, deviation, limit, shards=(), kind=jnp.bfloat16):
    values = jax.random.normal(stream_key, extent, jnp.float32) * deviation
    if len(shards) > 0:
        values = block_levels(stream_key, extent, shards, -0.22, 0.18) * values
    return jnp.clip(values, min=-limit, max=limit).astype(kind)


def setup_inputs(seed: int = 0, part: int = 0) -> dict:
    streams_of = jax.random.split(jax.random.key(seed), 9)
    own_keys = jax.random.split(jax.random.fold_in(streams_of[8], part), 9)
    return {
        "probes_spec": bell_draw(own_keys[0], (PROBES, LF, 2, MW, NN), 1.0, 6.0, ((0, 2), (3, 8))),
        "legendre": bell_draw(streams_of[1], (MW, LAT, NN), NN ** -0.5, 0.15625, ((0, 8),)),
        "wave_order": jax.random.permutation(streams_of[2], MW).astype(jnp.int32),
        "obs_weight": jnp.clip(jnp.exp(math.log(4.0) - 2.7725887 * jax.random.uniform(own_keys[3], (LFD, OBS), jnp.float32) ** block_levels(own_keys[3], (LFD, OBS), ((1, 8),), -0.2, 0.2)), 0.25, 4.0),
        "send_rows": draw_send_rows(jax.random.fold_in(jax.random.fold_in(streams_of[8], part), 71), part),
        "send_counts": draw_send_counts(jax.random.fold_in(jax.random.fold_in(streams_of[8], part), 71), part),
        "interp_idx": draw_interp_idx(jax.random.fold_in(jax.random.fold_in(streams_of[8], part), 71), part),
        "interp_weight": draw_interp_weight(jax.random.fold_in(jax.random.fold_in(streams_of[8], part), 71), part),
    }


def make_basis(wave_numbers):
    columns = jnp.arange(NLON, dtype=jnp.int32)
    phases = wave_numbers[:, None] * columns[None, :] % NLON
    angles = phases.astype(jnp.float32) * (2.0 * math.pi / NLON)
    factor = 1.0 / math.sqrt(MW)
    return jnp.stack([factor * jnp.cos(angles), -factor * jnp.sin(angles)]).astype(jnp.bfloat16)

def reference(probes_spec, legendre, wave_order, obs_weight, send_rows, send_counts, interp_idx, interp_weight):
    fourier_basis = make_basis(wave_order)
    basis_wide = fourier_basis.astype(jnp.float32)
    legendre_wide = legendre.astype(jnp.float32)
    slot_ids = jnp.arange(CAP, dtype=jnp.int32)
    live_mask = slot_ids[None, None, :] < send_counts[:, :, None]
    live_dest = jnp.transpose(live_mask, (1, 0, 2))
    owners = jnp.arange(NODES, dtype=jnp.int32)
    record = owners[:, None, None] * OBS_DEV + send_rows
    weight_slots = obs_weight[:, record]
    weight_dest = jnp.transpose(weight_slots, (2, 0, 1, 3))
    flat_index = jnp.transpose(interp_idx, (1, 0, 2, 3)).reshape(NODES, 4 * NODES * CAP)
    corner_weight = jnp.transpose(interp_weight, (1, 0, 2, 3))

    def scatter_one(indices, term_rows):
        return jnp.zeros((LFD, LAT_DEV * NLON), jnp.float32).at[:, indices].add(term_rows)

    def one_probe(spectrum):
        fourier = jnp.einsum('fksn,sln->fksl', spectrum.astype(jnp.float32), legendre_wide).astype(jnp.bfloat16)
        grid_values = jnp.einsum('fksl,ksj->flj', fourier.astype(jnp.float32), basis_wide)
        node_grid = grid_values.reshape(WAVES, LFD, BANDS, LAT_DEV * NLON)
        node_grid = jnp.transpose(node_grid, (2, 0, 1, 3)).reshape(NODES, LFD, LAT_DEV * NLON)
        values = jnp.take_along_axis(node_grid, flat_index[:, None, :], axis=2).reshape(NODES, LFD, 4, NODES, CAP)
        corner_sums = lax.optimization_barrier(jnp.sum(values * corner_weight[:, None], axis=2))
        observed = jnp.where(live_dest[:, None], corner_sums, 0.0).astype(jnp.bfloat16)
        observed = lax.optimization_barrier(observed)
        weighted = (weight_dest * observed.astype(jnp.float32)).astype(jnp.bfloat16)
        scattered = (corner_weight[:, None] * weighted.astype(jnp.float32)[:, :, None]).reshape(NODES, LFD, 4 * NODES * CAP)
        adjoint = jax.vmap(scatter_one)(flat_index, scattered)
        adjoint = adjoint.reshape(BANDS, WAVES, LFD, LAT_DEV, NLON)
        adjoint = jnp.transpose(adjoint, (1, 2, 0, 3, 4)).reshape(LF, LAT, NLON).astype(jnp.bfloat16)
        fourier_adjoint = jnp.einsum('flj,ksj->fksl', adjoint.astype(jnp.float32), basis_wide).astype(jnp.bfloat16)
        return jnp.einsum('fksl,sln->fksn', fourier_adjoint.astype(jnp.float32), legendre_wide).astype(jnp.bfloat16)
    return lax.map(one_probe, probes_spec)
```

```python
import functools
import math

import jax
import jax.numpy as jnp
from jax import lax
from jax.experimental import pallas as pl
from jax.experimental.pallas import tpu as pltpu
from jax.sharding import PartitionSpec as P

NLON = 1280
SB = 16
F32 = jnp.float32
BF16 = jnp.bfloat16
NT = (((1,), (1,)), ((), ()))
TN = (((0,), (0,)), ((), ()))


def dot(a, b, dims=(((1,), (0,)), ((), ()))):
    return lax.dot_general(a, b, dims, preferred_element_type=F32)


def iota(shape, dim):
    return lax.broadcasted_iota(jnp.int32, shape, dim)


def cos_sin(phase):
    quarter = jnp.floor(phase * (4.0 / NLON) + 0.5)
    x = (phase - quarter * (NLON // 4)) * (2.0 * math.pi / NLON)
    x2 = x * x
    s = x * (1.0 + x2 * (-1 / 6 + x2 * (1 / 120 + x2 * (-1 / 5040 + x2 * (1 / 362880)))))
    c = 1.0 + x2 * (-0.5 + x2 * (1 / 24 + x2 * (-1 / 720 + x2 * (1 / 40320))))
    turn = quarter - 4.0 * jnp.floor(quarter * 0.25)
    odd = (turn == 1.0) | (turn == 3.0)
    cos = jnp.where(odd, s, c) * jnp.where((turn == 1.0) | (turn == 2.0), -1.0, 1.0)
    sin = jnp.where(odd, c, s) * jnp.where(turn >= 2.0, -1.0, 1.0)
    return cos, sin


def selector(lat, items):
    shape = (lat * items, items * SB * lat)
    row, col = iota(shape, 0), iota(shape, 1)
    same = (row // items == col % lat) & (row % items == col // (SB * lat))
    return jnp.where(same, 1.0, 0.0).astype(BF16)


def exchange_kernel(
    bands, waves, probes_hbm, legendre_hbm, wave_ref, obs_ref, rows_ref, counts_ref, idx_ref,
    weight_ref, out_ref, probe_buf, leg_buf, spread, basis, corner, send_w, recv_w, slot_w,
    send_1, recv_1, send_2, recv_2, lanes, point, weights, probe_sem, leg_sem, tx_w, rx_w, tx_1,
    rx_1, tx_2, rx_2,
):
    nodes = bands * waves
    _, probe_local, field_count, _, _, degrees = probe_buf.shape
    blocks, _, lat, _ = leg_buf.shape
    slots = blocks * SB
    fields = field_count // waves
    items = probe_local * fields
    lat_local = lat // bands
    rows = lat_local * items
    capacity = rows_ref.shape[2]
    total = nodes * slots
    band, wave = lax.axis_index("band"), lax.axis_index("wave")
    me = band * waves + wave

    def where_is(node):
        return {"band": node // waves, "wave": node % waves}

    def peer(step):
        return lax.rem(me + step, nodes)

    def copies(send, recv, tx, rx):
        return [
            pltpu.make_async_remote_copy(
                src_ref=send.at[peer(step)],
                dst_ref=recv.at[me],
                send_sem=tx.at[step],
                recv_sem=rx.at[step],
                device_id=where_is(peer(step)),
                device_id_type=pl.DeviceIdType.MESH,
            )
            for step in range(1, nodes)
        ]

    def load(block):
        part = pl.ds(block * SB, SB)
        return (
            pltpu.make_async_copy(
                probes_hbm.at[:, :, :, part, :], probe_buf.at[block], probe_sem.at[block]
            ),
            pltpu.make_async_copy(legendre_hbm.at[part], leg_buf.at[block], leg_sem.at[block]),
        )

    for block in range(blocks):
        for one in load(block):
            one.start()
    barrier = pltpu.get_barrier_semaphore()
    for step in range(1, nodes):
        pl.semaphore_signal(
            barrier, inc=1, device_id=where_is(peer(step)), device_id_type=pl.DeviceIdType.MESH
        )

    obs = jnp.concatenate([obs_ref[...]] * probe_local, axis=0)
    high = obs.astype(BF16).astype(F32)
    middle = (obs - high).astype(BF16).astype(F32)
    split = jnp.concatenate([high, middle, obs - high - middle], axis=0).astype(BF16)
    record = rows_ref[0]
    for node in range(nodes):
        pick = iota((obs.shape[1], capacity), 0) == record[node : node + 1, :]
        found = dot(split, jnp.where(pick, 1.0, 0.0).astype(BF16))
        send_w[node] = found[2 * items :] + found[items : 2 * items] + found[:items]
    pl.semaphore_wait(barrier, nodes - 1)
    copies_w = copies(send_w, recv_w, tx_w, rx_w)
    for one in copies_w:
        one.start()
    recv_w[me] = send_w[me]

    counts = counts_ref[...].astype(F32)
    mine = jnp.sum(jnp.where(iota(counts.shape, 1) == me, counts, 0.0), axis=1, keepdims=True)
    live = iota((nodes, capacity), 1).astype(F32) < mine
    for i in range(4):
        live_weight = jnp.where(live, weight_ref[i, 0], 0.0)
        for node in range(nodes):
            at = slice(node * capacity, (node + 1) * capacity)
            weights[i : i + 1, at] = live_weight[node : node + 1]
    for i in range(2):
        for node in range(nodes):
            at = slice(node * capacity, (node + 1) * capacity)
            point[i : i + 1, at] = idx_ref[i, 0, node : node + 1, :].astype(F32)

    choose = selector(lat, items)

    @pl.loop(0, blocks)
    def _(block):
        for one in load(block):
            one.wait()
        product = dot(
            probe_buf[block].reshape(probe_local * field_count * 2 * SB, degrees),
            leg_buf[block].reshape(SB * lat, degrees),
            NT,
        )
        own = iota(product.shape, 0) % SB == iota(product.shape, 1) // lat
        product = jnp.where(own, product, 0.0).astype(BF16)
        for p in range(probe_local):
            for w in range(waves):
                for e in range(fields):
                    for k in range(2):
                        first = (((p * waves + w) * fields + e) * 2 + k) * SB
                        item = (p * fields + e) * SB * lat
                        spread[w, k, block, :, item : item + SB * lat] = product[first : first + SB]

    for w in range(waves):
        fourier = dot(choose, spread[w].reshape(2 * slots, items * SB * lat), NT).astype(BF16)
        for b in range(bands):
            send_1[b * waves + w] = fourier[b * rows : (b + 1) * rows]
    copies_1 = copies(send_1, recv_1, tx_1, rx_1)
    for one in copies_1:
        one.start()
    recv_1[me] = send_1[me]

    factor = 1.0 / math.sqrt(total)
    for lane in range(0, total, 128):
        order = wave_ref[:, lane : lane + 128].astype(F32)
        turn_c, turn_s = cos_sin(order * 128.0)

        @pl.loop(0, 2)
        def _(half):
            j = (iota((64, 128), 0) + half * 64).astype(F32)
            cos, sin = cos_sin(j * order)
            cos, sin = cos * factor, sin * factor
            for turn in range(NLON // 128):
                at = pl.ds(pl.multiple_of(half * 64, 64), 64)
                basis[turn, at, lane : lane + 128] = cos.astype(BF16)
                basis[turn, at, total + lane : total + lane + 128] = (-sin).astype(BF16)
                cos, sin = cos * turn_c - sin * turn_s, sin * turn_c + cos * turn_s

    row_of = jnp.floor((point[0:1, :] + 0.5) * (1.0 / NLON))
    west = point[0:1, :] - row_of * NLON
    east = point[1:2, :] - row_of * NLON
    west_weight, east_weight = [], []
    for l in range(lat_local):
        south, north = row_of == float(l), row_of == float(l - 1)
        west_weight.append(
            jnp.where(south, weights[0:1, :], jnp.where(north, weights[2:3, :], 0.0))
        )
        east_weight.append(
            jnp.where(south, weights[1:2, :], jnp.where(north, weights[3:4, :], 0.0))
        )

    @pl.loop(0, NLON // 64)
    def _(part):
        j = (iota((64, west.shape[1]), 0) + part * 64).astype(F32)
        at_west, at_east = j == west, j == east
        for l in range(lat_local):
            corner[l, part] = jnp.where(
                at_west, west_weight[l], jnp.where(at_east, east_weight[l], 0.0)
            ).astype(BF16)

    for one in copies_w:
        one.wait()
    for node in range(nodes):
        slot_w[:, node * capacity : (node + 1) * capacity] = recv_w[node]
    for one in copies_1:
        one.wait()
    for node in range(nodes):
        got = recv_1[node].astype(F32)
        for k in range(2):
            at = k * total + node * slots
            lanes[:, at : at + slots] = got[:, k * slots : (k + 1) * slots]
    table = basis[...].reshape(NLON, 2 * total)
    grid_values = dot(lanes[...].astype(BF16), table, NT)
    observed = jnp.zeros((2 * items, nodes * capacity), F32)
    for l in range(lat_local):
        here = grid_values[l * items : (l + 1) * items]
        both = jnp.concatenate([here, here - here.astype(BF16).astype(F32)], axis=0)
        observed += dot(both.astype(BF16), corner[l].reshape(NLON, nodes * capacity))
    observed = (observed[:items] + observed[items:]).astype(BF16).astype(F32)
    weighted = (slot_w[...] * observed).astype(BF16)
    adjoint = jnp.concatenate(
        [dot(weighted, corner[l].reshape(NLON, nodes * capacity), NT) for l in range(lat_local)],
        axis=0,
    ).astype(BF16)
    lanes[...] = dot(adjoint, table)
    for node in range(nodes):
        at = node * slots
        send_2[node] = jnp.concatenate(
            [lanes[:, at : at + slots], lanes[:, total + at : total + at + slots]], axis=1
        ).astype(BF16)
    copies_2 = copies(send_2, recv_2, tx_2, rx_2)
    for one in copies_2:
        one.start()
    recv_2[me] = send_2[me]
    for one in copies_2:
        one.wait()
    for b in range(bands):
        for w in range(waves):
            out_ref[w, b * rows : (b + 1) * rows, :] = recv_2[b * waves + w]


def synthesis_kernel(adjoint_ref, legendre_ref, out_ref, spread):
    probe_local, field_count, _, _, degrees = out_ref.shape
    waves = adjoint_ref.shape[0]
    fields = field_count // waves
    items = probe_local * fields
    lat = legendre_ref.shape[1]
    block = pl.program_id(0)

    @pl.when(block == 0)
    def _():
        choose = selector(lat, items)
        for w in range(waves):
            wide = dot(adjoint_ref[w], choose, TN)
            own = iota(wide.shape, 0) % SB == iota(wide.shape, 1) % (SB * lat) // lat
            spread[w] = jnp.where(own, wide, 0.0).astype(BF16).reshape(spread.shape[1:])

    pieces = []
    for p in range(probe_local):
        for w in range(waves):
            for e in range(fields):
                for k in range(2):
                    item = (p * fields + e) * SB * lat
                    pieces.append(spread[w, k, block, :, item : item + SB * lat])
    result = dot(
        jnp.concatenate(pieces, axis=0), legendre_ref[...].reshape(SB * lat, degrees)
    )
    out_ref[...] = result.astype(BF16).reshape(out_ref.shape)


def fits_kernels(probes_spec, legendre, wave_order, obs_weight, send_rows, bands, waves):
    probe_local, field_count, _, slots, degrees = probes_spec.shape
    lat = legendre.shape[1]
    items = probe_local * field_count // waves
    return (
        slots % SB == 0
        and lat == 16
        and degrees % 128 == 0
        and wave_order.shape[0] % 128 == 0
        and field_count % waves == 0
        and obs_weight.shape[0] * probe_local == items
        and items == 8
        and lat % bands == 0
        and lat // bands * items % 16 == 0
        and 1 < bands * waves <= 8
        and bands * waves * send_rows.shape[2] % 128 == 0
        and obs_weight.shape[1] <= 1024
    )


def in_kernels(
    probes_spec, legendre, wave_order, obs_weight, send_rows, send_counts, interp_idx, interp_weight
):
    bands = lax.axis_size("band")
    waves = lax.axis_size("wave")
    nodes = bands * waves
    probe_local, field_count, _, slots, degrees = probes_spec.shape
    lat = legendre.shape[1]
    blocks = slots // SB
    items = probe_local * field_count // waves
    rows = lat // bands * items
    total = wave_order.shape[0]
    capacity = send_rows.shape[2]
    wide = items * SB * lat
    vmem = pl.BlockSpec(memory_space=pltpu.VMEM)
    hbm = pl.BlockSpec(memory_space=pl.ANY)
    dma = pltpu.SemaphoreType.DMA
    adjoint = pl.pallas_call(
        functools.partial(exchange_kernel, bands, waves),
        out_shape=jax.ShapeDtypeStruct((waves, bands * rows, 2 * slots), BF16),
        in_specs=[hbm, hbm] + [vmem] * 6,
        out_specs=vmem,
        scratch_shapes=[
            pltpu.VMEM((blocks, probe_local, field_count, 2, SB, degrees), BF16),
            pltpu.VMEM((blocks, SB, lat, degrees), BF16),
            pltpu.VMEM((waves, 2, blocks, SB, wide), BF16),
            pltpu.VMEM((NLON // 128, 128, 2 * total), BF16),
            pltpu.VMEM((lat // bands, NLON // 64, 64, nodes * capacity), BF16),
            pltpu.VMEM((nodes, items, capacity), F32),
            pltpu.VMEM((nodes, items, capacity), F32),
            pltpu.VMEM((items, nodes * capacity), F32),
            pltpu.VMEM((nodes, rows, 2 * slots), BF16),
            pltpu.VMEM((nodes, rows, 2 * slots), BF16),
            pltpu.VMEM((nodes, rows, 2 * slots), BF16),
            pltpu.VMEM((nodes, rows, 2 * slots), BF16),
            pltpu.VMEM((rows, 2 * total), F32),
            pltpu.VMEM((8, nodes * capacity), F32),
            pltpu.VMEM((8, nodes * capacity), F32),
            dma((blocks,)),
            dma((blocks,)),
            dma((nodes,)),
            dma((nodes,)),
            dma((nodes,)),
            dma((nodes,)),
            dma((nodes,)),
            dma((nodes,)),
        ],
        compiler_params=pltpu.CompilerParams(
            collective_id=0, has_side_effects=True, vmem_limit_bytes=48 * 2**20
        ),
    )(
        probes_spec, legendre, wave_order.reshape(1, total), obs_weight, send_rows, send_counts,
        interp_idx, interp_weight,
    )
    return pl.pallas_call(
        synthesis_kernel,
        grid=(blocks,),
        out_shape=jax.ShapeDtypeStruct(probes_spec.shape, BF16),
        in_specs=[
            pl.BlockSpec(adjoint.shape, lambda i: (0, 0, 0)),
            pl.BlockSpec((SB, lat, degrees), lambda i: (i, 0, 0)),
        ],
        out_specs=pl.BlockSpec(
            (probe_local, field_count, 2, SB, degrees), lambda i: (0, 0, 0, i, 0)
        ),
        scratch_shapes=[pltpu.VMEM((waves, 2, blocks, SB, wide), BF16)],
        compiler_params=pltpu.CompilerParams(vmem_limit_bytes=40 * 2**20),
    )(adjoint, legendre)


def make_basis(wave_numbers, lon_count, wave_total):
    columns = jnp.arange(lon_count, dtype=jnp.int32)
    phases = wave_numbers[:, None] * columns[None, :] % lon_count
    angles = phases.astype(jnp.float32) * (2.0 * math.pi / lon_count)
    factor = 1.0 / math.sqrt(wave_total)
    return jnp.stack([factor * jnp.cos(angles), -factor * jnp.sin(angles)]).astype(jnp.bfloat16)


def in_general(
    probes_spec, legendre, wave_order, obs_weight, send_rows, send_counts, interp_idx, interp_weight
):
    band_count = lax.axis_size("band")
    wave_count = lax.axis_size("wave")
    node_count = band_count * wave_count
    probe_local, field_count, _, slot_local, degree_count = probes_spec.shape
    field_local = field_count // wave_count
    lat_local = legendre.shape[1] // band_count
    wave_total = wave_order.shape[0]
    capacity = send_rows.shape[2]
    points = lat_local * NLON
    spec_split = probes_spec.reshape(
        probe_local, wave_count, field_local, 2, slot_local, degree_count
    )
    legendre_split = legendre.reshape(slot_local, band_count, lat_local, degree_count)
    fourier = jnp.einsum(
        "pwgksn,sbln->bwpglks", spec_split, legendre_split, preferred_element_type=jnp.float32
    ).astype(jnp.bfloat16)
    fourier_basis = make_basis(wave_order, NLON, wave_total)
    flat_fourier = fourier.reshape(node_count, probe_local, field_local, lat_local, 2, slot_local)
    grid_values = jnp.einsum(
        "pglks,ksj->pglj",
        lax.all_to_all(flat_fourier, ("band", "wave"), split_axis=0, concat_axis=5, tiled=True)[0],
        fourier_basis,
        preferred_element_type=jnp.float32,
    )
    grid_flat = grid_values.reshape(probe_local, field_local, points)
    node_index = lax.axis_index(("band", "wave"))
    counts_here = lax.dynamic_slice_in_dim(send_counts, node_index, 1, 1)[:, 0]
    live_mask = jnp.arange(capacity, dtype=jnp.int32)[None, :] < counts_here[:, None]
    corner_index = interp_idx[:, 0].reshape(-1)
    corner_weight = interp_weight[:, 0]
    values = jnp.take(grid_flat, corner_index, axis=2).reshape(
        probe_local, field_local, 4, node_count, capacity
    )
    corner_sums = jnp.sum(values * corner_weight[None, None], axis=2)
    observed = jnp.where(live_mask[None, None], corner_sums, 0.0).astype(jnp.bfloat16)
    record_index = send_rows[0].reshape(-1)
    slot_weight = jnp.take(obs_weight, record_index, axis=1).reshape(
        field_local, node_count, capacity
    )
    scaled = (
        slot_weight[None]
        * lax.all_to_all(
            observed, ("band", "wave"), split_axis=2, concat_axis=2, tiled=True
        ).astype(jnp.float32)
    ).astype(jnp.bfloat16)
    weighted = lax.all_to_all(scaled, ("band", "wave"), split_axis=2, concat_axis=2, tiled=True)
    scattered = (corner_weight[None, None] * weighted.astype(jnp.float32)[:, :, None]).reshape(
        probe_local, field_local, -1
    )
    adjoint = (
        jnp.zeros((probe_local, field_local, points), jnp.float32)
        .at[:, :, corner_index]
        .add(scattered)
    )
    adjoint = adjoint.reshape(probe_local, field_local, lat_local, NLON).astype(jnp.bfloat16)
    fourier_adjoint = jnp.einsum(
        "pglj,ksj->pglks", adjoint, fourier_basis, preferred_element_type=jnp.float32
    ).astype(jnp.bfloat16)
    split_adjoint = fourier_adjoint.reshape(
        probe_local, field_local, lat_local, 2, node_count, slot_local
    )
    received = lax.all_to_all(
        split_adjoint, ("band", "wave"), split_axis=4, concat_axis=4, tiled=True
    )
    item_count = received.shape[0]
    parted = received.reshape(
        item_count, field_local, lat_local, 2, band_count, wave_count, slot_local
    )
    result = jnp.einsum(
        "pglkbws,sbln->pwgksn", parted, legendre_split, preferred_element_type=jnp.float32
    )
    return result.reshape(item_count, field_count, 2, slot_local, degree_count).astype(jnp.bfloat16)


def on_device(probes_spec, legendre, wave_order, obs_weight, send_rows, *others):
    sizes = lax.axis_size("band"), lax.axis_size("wave")
    fits = fits_kernels(probes_spec, legendre, wave_order, obs_weight, send_rows, *sizes)
    run = in_kernels if fits else in_general
    return run(probes_spec, legendre, wave_order, obs_weight, send_rows, *others)


def solution(mesh):
    placed = (
        P(("groups", "probe"), None, None, ("band", "wave"), None),
        P(("band", "wave"), None, None),
        P(),
        P(None, ("groups", "band", "wave")),
        P(("groups", "band", "wave"), None, None),
        P("groups", None),
        P(None, ("groups", "band", "wave"), None, None),
        P(None, ("groups", "band", "wave"), None, None),
    )
    return jax.shard_map(
        on_device,
        mesh=mesh,
        in_specs=placed,
        out_specs=P(("groups", "probe"), None, None, ("band", "wave"), None),
        check_vma=False,
    )
```

```python
import functools
import math

import jax
import jax.numpy as jnp
from jax import lax
from jax.experimental import pallas as pl
from jax.experimental.pallas import tpu as pltpu
from jax.sharding import PartitionSpec as P

NLON = 1280
SB = 16
F32 = jnp.float32
BF16 = jnp.bfloat16
NT = (((1,), (1,)), ((), ()))
TN = (((0,), (0,)), ((), ()))


def dot(a, b, dims=(((1,), (0,)), ((), ()))):
    return lax.dot_general(a, b, dims, preferred_element_type=F32)


def iota(shape, dim):
    return lax.broadcasted_iota(jnp.int32, shape, dim)


def cos_sin(phase):
    quarter = jnp.floor(phase * (4.0 / NLON) + 0.5)
    x = (phase - quarter * (NLON // 4)) * (2.0 * math.pi / NLON)
    x2 = x * x
    s = x * (1.0 + x2 * (-1 / 6 + x2 * (1 / 120 + x2 * (-1 / 5040 + x2 * (1 / 362880)))))
    c = 1.0 + x2 * (-0.5 + x2 * (1 / 24 + x2 * (-1 / 720 + x2 * (1 / 40320))))
    turn = quarter - 4.0 * jnp.floor(quarter * 0.25)
    odd = (turn == 1.0) | (turn == 3.0)
    cos = jnp.where(odd, s, c) * jnp.where((turn == 1.0) | (turn == 2.0), -1.0, 1.0)
    sin = jnp.where(odd, c, s) * jnp.where(turn >= 2.0, -1.0, 1.0)
    return cos, sin


def selector(lat, items):
    shape = (lat * items, items * SB * lat)
    row, col = iota(shape, 0), iota(shape, 1)
    item_bits, span_bits = items.bit_length() - 1, (SB * lat).bit_length() - 1
    same = (row >> item_bits == col & lat - 1) & (row & items - 1 == col >> span_bits)
    return jnp.where(same, 1.0, 0.0).astype(BF16)


def exchange_kernel(
    bands, waves, probes_hbm, legendre_hbm, wave_hbm, obs_hbm, rows_hbm, counts_hbm, idx_hbm,
    weight_hbm, out_ref, wave_ref, obs_ref, rows_ref, counts_ref, idx_ref, weight_ref, probe_buf, leg_buf, spread, basis, corner, send_w, recv_w, slot_w,
    send_1, recv_1, send_2, recv_2, lanes, point, weights, small_sem, probe_sem, leg_sem, tx_w, rx_w, tx_1,
    rx_1, tx_2, rx_2,
):
    nodes = bands * waves
    _, probe_local, field_count, _, _, degrees = probe_buf.shape
    blocks, _, lat, _ = leg_buf.shape
    slots = blocks * SB
    fields = field_count // waves
    items = probe_local * fields
    lat_local = lat // bands
    rows = lat_local * items
    capacity = rows_ref.shape[2]
    total = nodes * slots
    band, wave = lax.axis_index("band"), lax.axis_index("wave")
    me = band * waves + wave

    def where_is(node):
        return {"band": node // waves, "wave": node % waves}

    def peer(step):
        return lax.rem(me + step, nodes)

    def copies(send, recv, tx, rx):
        return [
            pltpu.make_async_remote_copy(
                src_ref=send.at[peer(step)],
                dst_ref=recv.at[me],
                send_sem=tx.at[step],
                recv_sem=rx.at[step],
                device_id=where_is(peer(step)),
                device_id_type=pl.DeviceIdType.MESH,
            )
            for step in range(1, nodes)
        ]

    def load(block):
        part = pl.ds(block * SB, SB)
        return (
            pltpu.make_async_copy(
                probes_hbm.at[:, :, :, part, :], probe_buf.at[block], probe_sem.at[block]
            ),
            pltpu.make_async_copy(legendre_hbm.at[part], leg_buf.at[block], leg_sem.at[block]),
        )

    smalls = [
        pltpu.make_async_copy(source, target, small_sem.at[i])
        for i, (source, target) in enumerate(
            (
                (obs_hbm, obs_ref),
                (rows_hbm, rows_ref),
                (counts_hbm, counts_ref),
                (idx_hbm, idx_ref),
                (weight_hbm, weight_ref),
                (wave_hbm, wave_ref),
            )
        )
    ]
    for block in range(blocks):
        for one in load(block):
            one.start()
    for one in smalls:
        one.start()
    barrier = pltpu.get_barrier_semaphore()
    for step in range(1, nodes):
        pl.semaphore_signal(
            barrier, inc=1, device_id=where_is(peer(step)), device_id_type=pl.DeviceIdType.MESH
        )

    choose = selector(lat, items)
    @pl.loop(0, blocks)
    def _(block):
        for one in load(block):
            one.wait()
        product = dot(
            probe_buf[block].reshape(probe_local * field_count * 2 * SB, degrees),
            leg_buf[block].reshape(SB * lat, degrees),
            NT,
        )
        own = iota(product.shape, 0) & SB - 1 == iota(product.shape, 1) >> lat.bit_length() - 1
        product = jnp.where(own, product, 0.0).astype(BF16)
        for p in range(probe_local):
            for w in range(waves):
                for e in range(fields):
                    for k in range(2):
                        first = (((p * waves + w) * fields + e) * 2 + k) * SB
                        item = (p * fields + e) * SB * lat
                        spread[w, k, block, :, item : item + SB * lat] = product[first : first + SB]

    for w in range(waves):
        fourier = dot(choose, spread[w].reshape(2 * slots, items * SB * lat), NT).astype(BF16)
        for b in range(bands):
            send_1[b * waves + w] = fourier[b * rows : (b + 1) * rows]
    pl.semaphore_wait(barrier, nodes - 1)
    copies_1 = copies(send_1, recv_1, tx_1, rx_1)
    for one in copies_1:
        one.start()
    recv_1[me] = send_1[me]

    for one in smalls:
        one.wait()

    obs = jnp.concatenate([obs_ref[...]] * probe_local, axis=0)
    high = obs.astype(BF16).astype(F32)
    middle = (obs - high).astype(BF16).astype(F32)
    split = jnp.concatenate([high, middle, obs - high - middle], axis=0).astype(BF16)
    record = rows_ref[0]
    for node in range(nodes):
        pick = iota((obs.shape[1], capacity), 0) == record[node : node + 1, :]
        found = dot(split, jnp.where(pick, 1.0, 0.0).astype(BF16))
        send_w[node] = found[2 * items :] + found[items : 2 * items] + found[:items]
    copies_w = copies(send_w, recv_w, tx_w, rx_w)
    for one in copies_w:
        one.start()
    recv_w[me] = send_w[me]

    counts = counts_ref[...].astype(F32)
    mine = jnp.sum(jnp.where(iota(counts.shape, 1) == me, counts, 0.0), axis=1, keepdims=True)
    live = iota((nodes, capacity), 1).astype(F32) < mine
    for i in range(4):
        live_weight = jnp.where(live, weight_ref[i, 0], 0.0)
        for node in range(nodes):
            at = slice(node * capacity, (node + 1) * capacity)
            weights[i : i + 1, at] = live_weight[node : node + 1]
    for i in range(2):
        for node in range(nodes):
            at = slice(node * capacity, (node + 1) * capacity)
            point[i : i + 1, at] = idx_ref[i, 0, node : node + 1, :].astype(F32)

    factor = 1.0 / math.sqrt(total)
    for lane in range(0, total, 128):
        order = wave_ref[lane : lane + 128].reshape(1, 128).astype(F32)
        turn_c, turn_s = cos_sin(order * 128.0)

        @pl.loop(0, 2)
        def _(half):
            j = (iota((64, 128), 0) + half * 64).astype(F32)
            cos, sin = cos_sin(j * order)
            cos, sin = cos * factor, sin * factor
            for turn in range(NLON // 128):
                at = pl.ds(pl.multiple_of(half * 64, 64), 64)
                basis[turn, at, lane : lane + 128] = cos.astype(BF16)
                basis[turn, at, total + lane : total + lane + 128] = (-sin).astype(BF16)
                cos, sin = cos * turn_c - sin * turn_s, sin * turn_c + cos * turn_s

    row_of = jnp.floor((point[0:1, :] + 0.5) * (1.0 / NLON))
    west = point[0:1, :] - row_of * NLON
    east = point[1:2, :] - row_of * NLON
    west_weight, east_weight = [], []
    for l in range(lat_local):
        south, north = row_of == float(l), row_of == float(l - 1)
        west_weight.append(
            jnp.where(south, weights[0:1, :], jnp.where(north, weights[2:3, :], 0.0))
        )
        east_weight.append(
            jnp.where(south, weights[1:2, :], jnp.where(north, weights[3:4, :], 0.0))
        )

    @pl.loop(0, NLON // 64)
    def _(part):
        j = (iota((64, west.shape[1]), 0) + part * 64).astype(F32)
        at_west, at_east = j == west, j == east
        for l in range(lat_local):
            corner[l, part] = jnp.where(
                at_west, west_weight[l], jnp.where(at_east, east_weight[l], 0.0)
            ).astype(BF16)

    for one in copies_w:
        one.wait()
    for node in range(nodes):
        slot_w[:, node * capacity : (node + 1) * capacity] = recv_w[node]
    for one in copies_1:
        one.wait()
    for node in range(nodes):
        got = recv_1[node].astype(F32)
        for k in range(2):
            at = k * total + node * slots
            lanes[:, at : at + slots] = got[:, k * slots : (k + 1) * slots]
    table = basis[...].reshape(NLON, 2 * total)
    grid_values = dot(lanes[...].astype(BF16), table, NT)
    observed = jnp.zeros((2 * items, nodes * capacity), F32)
    for l in range(lat_local):
        here = grid_values[l * items : (l + 1) * items]
        both = jnp.concatenate([here, here - here.astype(BF16).astype(F32)], axis=0)
        observed += dot(both.astype(BF16), corner[l].reshape(NLON, nodes * capacity))
    observed = (observed[:items] + observed[items:]).astype(BF16).astype(F32)
    weighted = (slot_w[...] * observed).astype(BF16)
    adjoint = jnp.concatenate(
        [dot(weighted, corner[l].reshape(NLON, nodes * capacity), NT) for l in range(lat_local)],
        axis=0,
    ).astype(BF16)
    lanes[...] = dot(adjoint, table)
    for node in range(nodes):
        at = node * slots
        send_2[node] = jnp.concatenate(
            [lanes[:, at : at + slots], lanes[:, total + at : total + at + slots]], axis=1
        ).astype(BF16)
    copies_2 = copies(send_2, recv_2, tx_2, rx_2)
    for one in copies_2:
        one.start()
    recv_2[me] = send_2[me]
    for one in copies_2:
        one.wait()
    for b in range(bands):
        for w in range(waves):
            out_ref[w, b * rows : (b + 1) * rows, :] = recv_2[b * waves + w]


def synthesis_kernel(adjoint_ref, legendre_ref, out_ref, spread):
    probe_local, field_count, _, _, degrees = out_ref.shape
    waves = adjoint_ref.shape[0]
    fields = field_count // waves
    items = probe_local * fields
    lat = legendre_ref.shape[1]
    block = pl.program_id(0)

    @pl.when(block == 0)
    def _():
        choose = selector(lat, items)
        for w in range(waves):
            wide = dot(adjoint_ref[w], choose, TN)
            column = iota(wide.shape, 1) & SB * lat - 1
            own = iota(wide.shape, 0) & SB - 1 == column >> lat.bit_length() - 1
            spread[w] = jnp.where(own, wide, 0.0).astype(BF16).reshape(spread.shape[1:])

    pieces = []
    for p in range(probe_local):
        for w in range(waves):
            for e in range(fields):
                for k in range(2):
                    item = (p * fields + e) * SB * lat
                    pieces.append(spread[w, k, block, :, item : item + SB * lat])
    result = dot(
        jnp.concatenate(pieces, axis=0), legendre_ref[...].reshape(SB * lat, degrees)
    )
    out_ref[...] = result.astype(BF16).reshape(out_ref.shape)


def fits_kernels(probes_spec, legendre, wave_order, obs_weight, send_rows, bands, waves):
    probe_local, field_count, _, slots, degrees = probes_spec.shape
    lat = legendre.shape[1]
    items = probe_local * field_count // waves
    return (
        slots % SB == 0
        and lat == 16
        and degrees % 128 == 0
        and wave_order.shape[0] % 128 == 0
        and field_count % waves == 0
        and obs_weight.shape[0] * probe_local == items
        and items == 8
        and lat % bands == 0
        and lat // bands * items % 16 == 0
        and 1 < bands * waves <= 8
        and bands * waves * send_rows.shape[2] % 128 == 0
        and obs_weight.shape[1] <= 1024
    )


def in_kernels(
    probes_spec, legendre, wave_order, obs_weight, send_rows, send_counts, interp_idx, interp_weight
):
    bands = lax.axis_size("band")
    waves = lax.axis_size("wave")
    nodes = bands * waves
    probe_local, field_count, _, slots, degrees = probes_spec.shape
    lat = legendre.shape[1]
    blocks = slots // SB
    items = probe_local * field_count // waves
    rows = lat // bands * items
    total = wave_order.shape[0]
    capacity = send_rows.shape[2]
    wide = items * SB * lat
    vmem = pl.BlockSpec(memory_space=pltpu.VMEM)
    hbm = pl.BlockSpec(memory_space=pltpu.HBM)
    dma = pltpu.SemaphoreType.DMA
    adjoint = pl.pallas_call(
        functools.partial(exchange_kernel, bands, waves),
        out_shape=jax.ShapeDtypeStruct((waves, bands * rows, 2 * slots), BF16),
        in_specs=[hbm] * 8,
        out_specs=vmem,
        scratch_shapes=[
            pltpu.VMEM(wave_order.shape, jnp.int32),
            pltpu.VMEM(obs_weight.shape, F32),
            pltpu.VMEM(send_rows.shape, jnp.int32),
            pltpu.VMEM(send_counts.shape, jnp.int32),
            pltpu.VMEM(interp_idx.shape, jnp.int32),
            pltpu.VMEM(interp_weight.shape, F32),
            pltpu.VMEM((blocks, probe_local, field_count, 2, SB, degrees), BF16),
            pltpu.VMEM((blocks, SB, lat, degrees), BF16),
            pltpu.VMEM((waves, 2, blocks, SB, wide), BF16),
            pltpu.VMEM((NLON // 128, 128, 2 * total), BF16),
            pltpu.VMEM((lat // bands, NLON // 64, 64, nodes * capacity), BF16),
            pltpu.VMEM((nodes, items, capacity), F32),
            pltpu.VMEM((nodes, items, capacity), F32),
            pltpu.VMEM((items, nodes * capacity), F32),
            pltpu.VMEM((nodes, rows, 2 * slots), BF16),
            pltpu.VMEM((nodes, rows, 2 * slots), BF16),
            pltpu.VMEM((nodes, rows, 2 * slots), BF16),
            pltpu.VMEM((nodes, rows, 2 * slots), BF16),
            pltpu.VMEM((rows, 2 * total), F32),
            pltpu.VMEM((8, nodes * capacity), F32),
            pltpu.VMEM((8, nodes * capacity), F32),
            dma((6,)),
            dma((blocks,)),
            dma((blocks,)),
            dma((nodes,)),
            dma((nodes,)),
            dma((nodes,)),
            dma((nodes,)),
            dma((nodes,)),
            dma((nodes,)),
        ],
        compiler_params=pltpu.CompilerParams(
            collective_id=0, has_side_effects=True, vmem_limit_bytes=64 * 2**20
        ),
    )(
        probes_spec, legendre, wave_order, obs_weight, send_rows, send_counts,
        interp_idx, interp_weight,
    )
    return pl.pallas_call(
        synthesis_kernel,
        grid=(blocks,),
        out_shape=jax.ShapeDtypeStruct(probes_spec.shape, BF16),
        in_specs=[
            pl.BlockSpec(adjoint.shape, lambda i: (0, 0, 0)),
            pl.BlockSpec((SB, lat, degrees), lambda i: (i, 0, 0)),
        ],
        out_specs=pl.BlockSpec(
            (probe_local, field_count, 2, SB, degrees), lambda i: (0, 0, 0, i, 0)
        ),
        scratch_shapes=[pltpu.VMEM((waves, 2, blocks, SB, wide), BF16)],
        compiler_params=pltpu.CompilerParams(vmem_limit_bytes=64 * 2**20),
    )(adjoint, legendre)


def make_basis(wave_numbers, lon_count, wave_total):
    columns = jnp.arange(lon_count, dtype=jnp.int32)
    phases = wave_numbers[:, None] * columns[None, :] % lon_count
    angles = phases.astype(jnp.float32) * (2.0 * math.pi / lon_count)
    factor = 1.0 / math.sqrt(wave_total)
    return jnp.stack([factor * jnp.cos(angles), -factor * jnp.sin(angles)]).astype(jnp.bfloat16)


def in_general(
    probes_spec, legendre, wave_order, obs_weight, send_rows, send_counts, interp_idx, interp_weight
):
    band_count = lax.axis_size("band")
    wave_count = lax.axis_size("wave")
    node_count = band_count * wave_count
    probe_local, field_count, _, slot_local, degree_count = probes_spec.shape
    field_local = field_count // wave_count
    lat_local = legendre.shape[1] // band_count
    wave_total = wave_order.shape[0]
    capacity = send_rows.shape[2]
    points = lat_local * NLON
    spec_split = probes_spec.reshape(
        probe_local, wave_count, field_local, 2, slot_local, degree_count
    )
    legendre_split = legendre.reshape(slot_local, band_count, lat_local, degree_count)
    fourier = jnp.einsum(
        "pwgksn,sbln->bwpglks", spec_split, legendre_split, preferred_element_type=jnp.float32
    ).astype(jnp.bfloat16)
    fourier_basis = make_basis(wave_order, NLON, wave_total)
    flat_fourier = fourier.reshape(node_count, probe_local, field_local, lat_local, 2, slot_local)
    grid_values = jnp.einsum(
        "pglks,ksj->pglj",
        lax.all_to_all(flat_fourier, ("band", "wave"), split_axis=0, concat_axis=5, tiled=True)[0],
        fourier_basis,
        preferred_element_type=jnp.float32,
    )
    grid_flat = grid_values.reshape(probe_local, field_local, points)
    node_index = lax.axis_index(("band", "wave"))
    counts_here = lax.dynamic_slice_in_dim(send_counts, node_index, 1, 1)[:, 0]
    live_mask = jnp.arange(capacity, dtype=jnp.int32)[None, :] < counts_here[:, None]
    corner_index = interp_idx[:, 0].reshape(-1)
    corner_weight = interp_weight[:, 0]
    values = jnp.take(grid_flat, corner_index, axis=2).reshape(
        probe_local, field_local, 4, node_count, capacity
    )
    corner_sums = jnp.sum(values * corner_weight[None, None], axis=2)
    observed = jnp.where(live_mask[None, None], corner_sums, 0.0).astype(jnp.bfloat16)
    record_index = send_rows[0].reshape(-1)
    slot_weight = jnp.take(obs_weight, record_index, axis=1).reshape(
        field_local, node_count, capacity
    )
    scaled = (
        slot_weight[None]
        * lax.all_to_all(
            observed, ("band", "wave"), split_axis=2, concat_axis=2, tiled=True
        ).astype(jnp.float32)
    ).astype(jnp.bfloat16)
    weighted = lax.all_to_all(scaled, ("band", "wave"), split_axis=2, concat_axis=2, tiled=True)
    scattered = (corner_weight[None, None] * weighted.astype(jnp.float32)[:, :, None]).reshape(
        probe_local, field_local, -1
    )
    adjoint = (
        jnp.zeros((probe_local, field_local, points), jnp.float32)
        .at[:, :, corner_index]
        .add(scattered)
    )
    adjoint = adjoint.reshape(probe_local, field_local, lat_local, NLON).astype(jnp.bfloat16)
    fourier_adjoint = jnp.einsum(
        "pglj,ksj->pglks", adjoint, fourier_basis, preferred_element_type=jnp.float32
    ).astype(jnp.bfloat16)
    split_adjoint = fourier_adjoint.reshape(
        probe_local, field_local, lat_local, 2, node_count, slot_local
    )
    received = lax.all_to_all(
        split_adjoint, ("band", "wave"), split_axis=4, concat_axis=4, tiled=True
    )
    item_count = received.shape[0]
    parted = received.reshape(
        item_count, field_local, lat_local, 2, band_count, wave_count, slot_local
    )
    result = jnp.einsum(
        "pglkbws,sbln->pwgksn", parted, legendre_split, preferred_element_type=jnp.float32
    )
    return result.reshape(item_count, field_count, 2, slot_local, degree_count).astype(jnp.bfloat16)


def on_device(probes_spec, legendre, wave_order, obs_weight, send_rows, *others):
    sizes = lax.axis_size("band"), lax.axis_size("wave")
    fits = fits_kernels(probes_spec, legendre, wave_order, obs_weight, send_rows, *sizes)
    run = in_kernels if fits else in_general
    return run(probes_spec, legendre, wave_order, obs_weight, send_rows, *others)


def solution(mesh):
    placed = (
        P(("groups", "probe"), None, None, ("band", "wave"), None),
        P(("band", "wave"), None, None),
        P(),
        P(None, ("groups", "band", "wave")),
        P(("groups", "band", "wave"), None, None),
        P("groups", None),
        P(None, ("groups", "band", "wave"), None, None),
        P(None, ("groups", "band", "wave"), None, None),
    )
    return jax.shard_map(
        on_device,
        mesh=mesh,
        in_specs=placed,
        out_specs=P(("groups", "probe"), None, None, ("band", "wave"), None),
        check_vma=False,
    )
```

```python
import functools
import math

import jax
import jax.numpy as jnp
from jax import lax
from jax.experimental import pallas as pl
from jax.experimental.pallas import tpu as pltpu
from jax.sharding import PartitionSpec as P

NLON = 1280
SB = 16
F32 = jnp.float32
BF16 = jnp.bfloat16
NT = (((1,), (1,)), ((), ()))
TN = (((0,), (0,)), ((), ()))


def dot(a, b, dims=(((1,), (0,)), ((), ()))):
    return lax.dot_general(a, b, dims, preferred_element_type=F32)


def iota(shape, dim):
    return lax.broadcasted_iota(jnp.int32, shape, dim)


def cos_sin(phase):
    quarter = jnp.floor(phase * (4.0 / NLON) + 0.5)
    x = (phase - quarter * (NLON // 4)) * (2.0 * math.pi / NLON)
    x2 = x * x
    s = x * (1.0 + x2 * (-1 / 6 + x2 * (1 / 120 + x2 * (-1 / 5040 + x2 * (1 / 362880)))))
    c = 1.0 + x2 * (-0.5 + x2 * (1 / 24 + x2 * (-1 / 720 + x2 * (1 / 40320))))
    turn = quarter - 4.0 * jnp.floor(quarter * 0.25)
    odd = (turn == 1.0) | (turn == 3.0)
    cos = jnp.where(odd, s, c) * jnp.where((turn == 1.0) | (turn == 2.0), -1.0, 1.0)
    sin = jnp.where(odd, c, s) * jnp.where(turn >= 2.0, -1.0, 1.0)
    return cos, sin


def selector(lat, items):
    shape = (lat * items, items * SB * lat)
    row, col = iota(shape, 0), iota(shape, 1)
    item_bits, span_bits = items.bit_length() - 1, (SB * lat).bit_length() - 1
    same = (row >> item_bits == col & lat - 1) & (row & items - 1 == col >> span_bits)
    return jnp.where(same, 1.0, 0.0).astype(BF16)


def exchange_kernel(
    bands, waves, probes_hbm, legendre_hbm, wave_hbm, obs_hbm, rows_hbm, counts_hbm, idx_hbm,
    weight_hbm, out_ref, wave_ref, obs_ref, rows_ref, counts_ref, idx_ref, weight_ref, probe_buf, leg_buf, spread, basis, corner, send_w, recv_w, slot_w,
    send_1, recv_1, send_2, recv_2, lanes, point, weights, small_sem, probe_sem, leg_sem, tx_w, rx_w, tx_1,
    rx_1, tx_2, rx_2,
):
    nodes = bands * waves
    _, probe_local, field_count, _, _, degrees = probe_buf.shape
    blocks, _, lat, _ = leg_buf.shape
    slots = blocks * SB
    fields = field_count // waves
    items = probe_local * fields
    lat_local = lat // bands
    rows = lat_local * items
    capacity = rows_ref.shape[2]
    total = nodes * slots
    band, wave = lax.axis_index("band"), lax.axis_index("wave")
    me = band * waves + wave

    def where_is(node):
        return {"band": node // waves, "wave": node % waves}

    def peer(step):
        return lax.rem(me + step, nodes)

    def copies(send, recv, tx, rx):
        return [
            pltpu.make_async_remote_copy(
                src_ref=send.at[peer(step)],
                dst_ref=recv.at[me],
                send_sem=tx.at[step],
                recv_sem=rx.at[step],
                device_id=where_is(peer(step)),
                device_id_type=pl.DeviceIdType.MESH,
            )
            for step in range(1, nodes)
        ]

    def load(block):
        part = pl.ds(block * SB, SB)
        return (
            pltpu.make_async_copy(
                probes_hbm.at[:, :, :, part, :], probe_buf.at[block], probe_sem.at[block]
            ),
            pltpu.make_async_copy(legendre_hbm.at[part], leg_buf.at[block], leg_sem.at[block]),
        )

    smalls = [
        pltpu.make_async_copy(source, target, small_sem.at[i])
        for i, (source, target) in enumerate(
            (
                (obs_hbm, obs_ref),
                (rows_hbm, rows_ref),
                (counts_hbm, counts_ref),
                (idx_hbm, idx_ref),
                (weight_hbm, weight_ref),
                (wave_hbm, wave_ref),
            )
        )
    ]
    for block in range(blocks):
        for one in load(block):
            one.start()
    for one in smalls:
        one.start()
    barrier = pltpu.get_barrier_semaphore()
    for step in range(1, nodes):
        pl.semaphore_signal(
            barrier, inc=1, device_id=where_is(peer(step)), device_id_type=pl.DeviceIdType.MESH
        )

    choose = selector(lat, items)
    @pl.loop(0, blocks)
    def _(block):
        for one in load(block):
            one.wait()
        product = dot(
            probe_buf[block].reshape(probe_local * field_count * 2 * SB, degrees),
            leg_buf[block].reshape(SB * lat, degrees),
            NT,
        )
        own = iota(product.shape, 0) & SB - 1 == iota(product.shape, 1) >> lat.bit_length() - 1
        product = jnp.where(own, product, 0.0).astype(BF16)
        for p in range(probe_local):
            for w in range(waves):
                for e in range(fields):
                    for k in range(2):
                        first = (((p * waves + w) * fields + e) * 2 + k) * SB
                        item = (p * fields + e) * SB * lat
                        spread[w, k, block, :, item : item + SB * lat] = product[first : first + SB]

    for w in range(waves):
        fourier = dot(choose, spread[w].reshape(2 * slots, items * SB * lat), NT).astype(BF16)
        for b in range(bands):
            send_1[b * waves + w] = fourier[b * rows : (b + 1) * rows]
    pl.semaphore_wait(barrier, nodes - 1)
    copies_1 = copies(send_1, recv_1, tx_1, rx_1)
    for one in copies_1:
        one.start()
    recv_1[me] = send_1[me]

    for one in smalls:
        one.wait()

    obs = jnp.concatenate([obs_ref[...]] * probe_local, axis=0)
    high = obs.astype(BF16).astype(F32)
    middle = (obs - high).astype(BF16).astype(F32)
    split = jnp.concatenate([high, middle, obs - high - middle], axis=0).astype(BF16)
    record = rows_ref[0]
    for node in range(nodes):
        pick = iota((obs.shape[1], capacity), 0) == record[node : node + 1, :]
        found = dot(split, jnp.where(pick, 1.0, 0.0).astype(BF16))
        send_w[node] = found[2 * items :] + found[items : 2 * items] + found[:items]
    copies_w = copies(send_w, recv_w, tx_w, rx_w)
    for one in copies_w:
        one.start()
    recv_w[me] = send_w[me]

    counts = counts_ref[...].astype(F32)
    mine = jnp.sum(jnp.where(iota(counts.shape, 1) == me, counts, 0.0), axis=1, keepdims=True)
    live = iota((nodes, capacity), 1).astype(F32) < mine
    for i in range(4):
        live_weight = jnp.where(live, weight_ref[i, 0], 0.0)
        for node in range(nodes):
            at = slice(node * capacity, (node + 1) * capacity)
            weights[i : i + 1, at] = live_weight[node : node + 1]
    for i in range(2):
        for node in range(nodes):
            at = slice(node * capacity, (node + 1) * capacity)
            point[i : i + 1, at] = idx_ref[i, 0, node : node + 1, :].astype(F32)

    factor = 1.0 / math.sqrt(total)
    for lane in range(0, total, 128):
        order = wave_ref[lane : lane + 128].reshape(1, 128).astype(F32)
        turn_c, turn_s = cos_sin(order * 128.0)

        @pl.loop(0, 2)
        def _(half):
            j = (iota((64, 128), 0) + half * 64).astype(F32)
            cos, sin = cos_sin(j * order)
            cos, sin = cos * factor, sin * factor
            for turn in range(NLON // 128):
                at = pl.ds(pl.multiple_of(half * 64, 64), 64)
                basis[turn, at, lane : lane + 128] = cos.astype(BF16)
                basis[turn, at, total + lane : total + lane + 128] = (-sin).astype(BF16)
                cos, sin = cos * turn_c - sin * turn_s, sin * turn_c + cos * turn_s

    row_of = jnp.floor((point[0:1, :] + 0.5) * (1.0 / NLON))
    west = point[0:1, :] - row_of * NLON
    east = point[1:2, :] - row_of * NLON
    west_weight, east_weight = [], []
    for l in range(lat_local):
        south, north = row_of == float(l), row_of == float(l - 1)
        west_weight.append(
            jnp.where(south, weights[0:1, :], jnp.where(north, weights[2:3, :], 0.0))
        )
        east_weight.append(
            jnp.where(south, weights[1:2, :], jnp.where(north, weights[3:4, :], 0.0))
        )

    @pl.loop(0, NLON // 64)
    def _(part):
        j = (iota((64, west.shape[1]), 0) + part * 64).astype(F32)
        at_west, at_east = j == west, j == east
        for l in range(lat_local):
            corner[l, part] = jnp.where(
                at_west, west_weight[l], jnp.where(at_east, east_weight[l], 0.0)
            ).astype(BF16)

    for one in copies_w:
        one.wait()
    for node in range(nodes):
        slot_w[:, node * capacity : (node + 1) * capacity] = recv_w[node]
    for one in copies_1:
        one.wait()
    for node in range(nodes):
        got = recv_1[node].astype(F32)
        for k in range(2):
            at = k * total + node * slots
            lanes[:, at : at + slots] = got[:, k * slots : (k + 1) * slots]
    table = basis[...].reshape(NLON, 2 * total)
    grid_values = dot(lanes[...].astype(BF16), table, NT)
    observed = jnp.zeros((2 * items, nodes * capacity), F32)
    for l in range(lat_local):
        here = grid_values[l * items : (l + 1) * items]
        both = jnp.concatenate([here, here - here.astype(BF16).astype(F32)], axis=0)
        observed += dot(both.astype(BF16), corner[l].reshape(NLON, nodes * capacity))
    observed = (observed[:items] + observed[items:]).astype(BF16).astype(F32)
    weighted = (slot_w[...] * observed).astype(BF16)
    adjoint = jnp.concatenate(
        [dot(weighted, corner[l].reshape(NLON, nodes * capacity), NT) for l in range(lat_local)],
        axis=0,
    ).astype(BF16)
    lanes[...] = dot(adjoint, table)
    for node in range(nodes):
        at = node * slots
        send_2[node] = jnp.concatenate(
            [lanes[:, at : at + slots], lanes[:, total + at : total + at + slots]], axis=1
        ).astype(BF16)
    copies_2 = copies(send_2, recv_2, tx_2, rx_2)
    for one in copies_2:
        one.start()
    recv_2[me] = send_2[me]
    for one in copies_2:
        one.wait()
    for b in range(bands):
        for w in range(waves):
            out_ref[w, b * rows : (b + 1) * rows, :] = recv_2[b * waves + w]


def synthesis_kernel(adjoint_ref, legendre_ref, out_ref, spread):
    probe_local, field_count, _, _, degrees = out_ref.shape
    waves = adjoint_ref.shape[0]
    fields = field_count // waves
    items = probe_local * fields
    lat = legendre_ref.shape[1]
    block = pl.program_id(0)

    @pl.when(block == 0)
    def _():
        choose = selector(lat, items)
        for w in range(waves):
            wide = dot(adjoint_ref[w], choose, TN)
            column = iota(wide.shape, 1) & SB * lat - 1
            own = iota(wide.shape, 0) & SB - 1 == column >> lat.bit_length() - 1
            spread[w] = jnp.where(own, wide, 0.0).astype(BF16).reshape(spread.shape[1:])

    pieces = []
    for p in range(probe_local):
        for w in range(waves):
            for e in range(fields):
                for k in range(2):
                    item = (p * fields + e) * SB * lat
                    pieces.append(spread[w, k, block, :, item : item + SB * lat])
    result = dot(
        jnp.concatenate(pieces, axis=0), legendre_ref[...].reshape(SB * lat, degrees)
    )
    out_ref[...] = result.astype(BF16).reshape(out_ref.shape)


def fits_kernels(probes_spec, legendre, wave_order, obs_weight, send_rows, bands, waves):
    probe_local, field_count, _, slots, degrees = probes_spec.shape
    lat = legendre.shape[1]
    items = probe_local * field_count // waves
    return (
        slots % SB == 0
        and lat == 16
        and degrees % 128 == 0
        and wave_order.shape[0] % 128 == 0
        and field_count % waves == 0
        and obs_weight.shape[0] * probe_local == items
        and items == 8
        and lat % bands == 0
        and lat // bands * items % 16 == 0
        and 1 < bands * waves <= 8
        and bands * waves * send_rows.shape[2] % 128 == 0
        and obs_weight.shape[1] <= 1024
    )


def in_kernels(
    probes_spec, legendre, wave_order, obs_weight, send_rows, send_counts, interp_idx, interp_weight
):
    bands = lax.axis_size("band")
    waves = lax.axis_size("wave")
    nodes = bands * waves
    probe_local, field_count, _, slots, degrees = probes_spec.shape
    lat = legendre.shape[1]
    blocks = slots // SB
    items = probe_local * field_count // waves
    rows = lat // bands * items
    total = wave_order.shape[0]
    capacity = send_rows.shape[2]
    wide = items * SB * lat
    vmem = pl.BlockSpec(memory_space=pltpu.VMEM)
    hbm = pl.BlockSpec(memory_space=pltpu.HBM)
    dma = pltpu.SemaphoreType.DMA
    adjoint = pl.pallas_call(
        functools.partial(exchange_kernel, bands, waves),
        out_shape=jax.ShapeDtypeStruct((waves, bands * rows, 2 * slots), BF16),
        in_specs=[hbm] * 8,
        out_specs=vmem,
        scratch_shapes=[
            pltpu.VMEM(wave_order.shape, jnp.int32),
            pltpu.VMEM(obs_weight.shape, F32),
            pltpu.VMEM(send_rows.shape, jnp.int32),
            pltpu.VMEM(send_counts.shape, jnp.int32),
            pltpu.VMEM(interp_idx.shape, jnp.int32),
            pltpu.VMEM(interp_weight.shape, F32),
            pltpu.VMEM((blocks, probe_local, field_count, 2, SB, degrees), BF16),
            pltpu.VMEM((blocks, SB, lat, degrees), BF16),
            pltpu.VMEM((waves, 2, blocks, SB, wide), BF16),
            pltpu.VMEM((NLON // 128, 128, 2 * total), BF16),
            pltpu.VMEM((lat // bands, NLON // 64, 64, nodes * capacity), BF16),
            pltpu.VMEM((nodes, items, capacity), F32),
            pltpu.VMEM((nodes, items, capacity), F32),
            pltpu.VMEM((items, nodes * capacity), F32),
            pltpu.VMEM((nodes, rows, 2 * slots), BF16),
            pltpu.VMEM((nodes, rows, 2 * slots), BF16),
            pltpu.VMEM((nodes, rows, 2 * slots), BF16),
            pltpu.VMEM((nodes, rows, 2 * slots), BF16),
            pltpu.VMEM((rows, 2 * total), F32),
            pltpu.VMEM((8, nodes * capacity), F32),
            pltpu.VMEM((8, nodes * capacity), F32),
            dma((6,)),
            dma((blocks,)),
            dma((blocks,)),
            dma((nodes,)),
            dma((nodes,)),
            dma((nodes,)),
            dma((nodes,)),
            dma((nodes,)),
            dma((nodes,)),
        ],
        compiler_params=pltpu.CompilerParams(
            collective_id=0, has_side_effects=True, vmem_limit_bytes=40 * 2**20
        ),
    )(
        *(
            pltpu.with_memory_space_constraint(one, pltpu.HBM)
            for one in (
                probes_spec, legendre, wave_order, obs_weight, send_rows, send_counts, interp_idx,
                interp_weight,
            )
        )
    )
    return pl.pallas_call(
        synthesis_kernel,
        grid=(blocks,),
        out_shape=jax.ShapeDtypeStruct(probes_spec.shape, BF16),
        in_specs=[
            pl.BlockSpec(adjoint.shape, lambda i: (0, 0, 0)),
            pl.BlockSpec((SB, lat, degrees), lambda i: (i, 0, 0)),
        ],
        out_specs=pl.BlockSpec(
            (probe_local, field_count, 2, SB, degrees), lambda i: (0, 0, 0, i, 0)
        ),
        scratch_shapes=[pltpu.VMEM((waves, 2, blocks, SB, wide), BF16)],
        compiler_params=pltpu.CompilerParams(vmem_limit_bytes=40 * 2**20),
    )(adjoint, legendre)


def make_basis(wave_numbers, lon_count, wave_total):
    columns = jnp.arange(lon_count, dtype=jnp.int32)
    phases = wave_numbers[:, None] * columns[None, :] % lon_count
    angles = phases.astype(jnp.float32) * (2.0 * math.pi / lon_count)
    factor = 1.0 / math.sqrt(wave_total)
    return jnp.stack([factor * jnp.cos(angles), -factor * jnp.sin(angles)]).astype(jnp.bfloat16)


def in_general(
    probes_spec, legendre, wave_order, obs_weight, send_rows, send_counts, interp_idx, interp_weight
):
    band_count = lax.axis_size("band")
    wave_count = lax.axis_size("wave")
    node_count = band_count * wave_count
    probe_local, field_count, _, slot_local, degree_count = probes_spec.shape
    field_local = field_count // wave_count
    lat_local = legendre.shape[1] // band_count
    wave_total = wave_order.shape[0]
    capacity = send_rows.shape[2]
    points = lat_local * NLON
    spec_split = probes_spec.reshape(
        probe_local, wave_count, field_local, 2, slot_local, degree_count
    )
    legendre_split = legendre.reshape(slot_local, band_count, lat_local, degree_count)
    fourier = jnp.einsum(
        "pwgksn,sbln->bwpglks", spec_split, legendre_split, preferred_element_type=jnp.float32
    ).astype(jnp.bfloat16)
    fourier_basis = make_basis(wave_order, NLON, wave_total)
    flat_fourier = fourier.reshape(node_count, probe_local, field_local, lat_local, 2, slot_local)
    grid_values = jnp.einsum(
        "pglks,ksj->pglj",
        lax.all_to_all(flat_fourier, ("band", "wave"), split_axis=0, concat_axis=5, tiled=True)[0],
        fourier_basis,
        preferred_element_type=jnp.float32,
    )
    grid_flat = grid_values.reshape(probe_local, field_local, points)
    node_index = lax.axis_index(("band", "wave"))
    counts_here = lax.dynamic_slice_in_dim(send_counts, node_index, 1, 1)[:, 0]
    live_mask = jnp.arange(capacity, dtype=jnp.int32)[None, :] < counts_here[:, None]
    corner_index = interp_idx[:, 0].reshape(-1)
    corner_weight = interp_weight[:, 0]
    values = jnp.take(grid_flat, corner_index, axis=2).reshape(
        probe_local, field_local, 4, node_count, capacity
    )
    corner_sums = jnp.sum(values * corner_weight[None, None], axis=2)
    observed = jnp.where(live_mask[None, None], corner_sums, 0.0).astype(jnp.bfloat16)
    record_index = send_rows[0].reshape(-1)
    slot_weight = jnp.take(obs_weight, record_index, axis=1).reshape(
        field_local, node_count, capacity
    )
    scaled = (
        slot_weight[None]
        * lax.all_to_all(
            observed, ("band", "wave"), split_axis=2, concat_axis=2, tiled=True
        ).astype(jnp.float32)
    ).astype(jnp.bfloat16)
    weighted = lax.all_to_all(scaled, ("band", "wave"), split_axis=2, concat_axis=2, tiled=True)
    scattered = (corner_weight[None, None] * weighted.astype(jnp.float32)[:, :, None]).reshape(
        probe_local, field_local, -1
    )
    adjoint = (
        jnp.zeros((probe_local, field_local, points), jnp.float32)
        .at[:, :, corner_index]
        .add(scattered)
    )
    adjoint = adjoint.reshape(probe_local, field_local, lat_local, NLON).astype(jnp.bfloat16)
    fourier_adjoint = jnp.einsum(
        "pglj,ksj->pglks", adjoint, fourier_basis, preferred_element_type=jnp.float32
    ).astype(jnp.bfloat16)
    split_adjoint = fourier_adjoint.reshape(
        probe_local, field_local, lat_local, 2, node_count, slot_local
    )
    received = lax.all_to_all(
        split_adjoint, ("band", "wave"), split_axis=4, concat_axis=4, tiled=True
    )
    item_count = received.shape[0]
    parted = received.reshape(
        item_count, field_local, lat_local, 2, band_count, wave_count, slot_local
    )
    result = jnp.einsum(
        "pglkbws,sbln->pwgksn", parted, legendre_split, preferred_element_type=jnp.float32
    )
    return result.reshape(item_count, field_count, 2, slot_local, degree_count).astype(jnp.bfloat16)


def on_device(probes_spec, legendre, wave_order, obs_weight, send_rows, *others):
    sizes = lax.axis_size("band"), lax.axis_size("wave")
    fits = fits_kernels(probes_spec, legendre, wave_order, obs_weight, send_rows, *sizes)
    run = in_kernels if fits else in_general
    return run(probes_spec, legendre, wave_order, obs_weight, send_rows, *others)


def solution(mesh):
    placed = (
        P(("groups", "probe"), None, None, ("band", "wave"), None),
        P(("band", "wave"), None, None),
        P(),
        P(None, ("groups", "band", "wave")),
        P(("groups", "band", "wave"), None, None),
        P("groups", None),
        P(None, ("groups", "band", "wave"), None, None),
        P(None, ("groups", "band", "wave"), None, None),
    )
    return jax.shard_map(
        on_device,
        mesh=mesh,
        in_specs=placed,
        out_specs=P(("groups", "probe"), None, None, ("band", "wave"), None),
        check_vma=False,
    )
```

```python
import functools
import math

import jax
import jax.numpy as jnp
from jax import lax
from jax.experimental import pallas as pl
from jax.experimental.pallas import tpu as pltpu
from jax.sharding import PartitionSpec as P

NLON = 1280
SB = 16
F32 = jnp.float32
BF16 = jnp.bfloat16
NT = (((1,), (1,)), ((), ()))
TN = (((0,), (0,)), ((), ()))


def dot(a, b, dims=(((1,), (0,)), ((), ()))):
    return lax.dot_general(a, b, dims, preferred_element_type=F32)


def iota(shape, dim):
    return lax.broadcasted_iota(jnp.int32, shape, dim)


def cos_sin(phase):
    quarter = jnp.floor(phase * (4.0 / NLON) + 0.5)
    x = (phase - quarter * (NLON // 4)) * (2.0 * math.pi / NLON)
    x2 = x * x
    s = x * (1.0 + x2 * (-1 / 6 + x2 * (1 / 120 + x2 * (-1 / 5040 + x2 * (1 / 362880)))))
    c = 1.0 + x2 * (-0.5 + x2 * (1 / 24 + x2 * (-1 / 720 + x2 * (1 / 40320))))
    turn = quarter - 4.0 * jnp.floor(quarter * 0.25)
    odd = (turn == 1.0) | (turn == 3.0)
    cos = jnp.where(odd, s, c) * jnp.where((turn == 1.0) | (turn == 2.0), -1.0, 1.0)
    sin = jnp.where(odd, c, s) * jnp.where(turn >= 2.0, -1.0, 1.0)
    return cos, sin


def selector(lat, items):
    shape = (lat * items, items * SB * lat)
    row, col = iota(shape, 0), iota(shape, 1)
    item_bits, span_bits = items.bit_length() - 1, (SB * lat).bit_length() - 1
    same = (row >> item_bits == col & lat - 1) & (row & items - 1 == col >> span_bits)
    return jnp.where(same, 1.0, 0.0).astype(BF16)


def own_slot(lat):
    shape = (SB, SB * lat)
    return iota(shape, 0) == iota(shape, 1) >> lat.bit_length() - 1


def exchange_kernel(
    bands, waves, probes_hbm, legendre_hbm, wave_hbm, obs_hbm, rows_hbm, counts_hbm, idx_hbm,
    weight_hbm, out_ref, wave_ref, obs_ref, rows_ref, counts_ref, idx_ref, weight_ref, probe_buf, leg_buf, spread, basis, corner, send_w, recv_w, slot_w,
    send_1, recv_1, send_2, recv_2, lanes, point, weights, small_sem, probe_sem, leg_sem, tx_w, rx_w, tx_1,
    rx_1, tx_2, rx_2,
):
    nodes = bands * waves
    _, probe_local, field_count, _, _, degrees = probe_buf.shape
    blocks, _, lat, _ = leg_buf.shape
    slots = blocks * SB
    fields = field_count // waves
    items = probe_local * fields
    lat_local = lat // bands
    rows = lat_local * items
    capacity = rows_ref.shape[2]
    total = nodes * slots
    band, wave = lax.axis_index("band"), lax.axis_index("wave")
    me = band * waves + wave

    def where_is(node):
        return {"band": node // waves, "wave": node % waves}

    def peer(step):
        return lax.rem(me + step, nodes)

    def copies(send, recv, tx, rx):
        return [
            pltpu.make_async_remote_copy(
                src_ref=send.at[peer(step)],
                dst_ref=recv.at[me],
                send_sem=tx.at[step],
                recv_sem=rx.at[step],
                device_id=where_is(peer(step)),
                device_id_type=pl.DeviceIdType.MESH,
            )
            for step in range(1, nodes)
        ]

    def load(block):
        part = pl.ds(block * SB, SB)
        return (
            pltpu.make_async_copy(
                probes_hbm.at[:, :, :, part, :], probe_buf.at[block], probe_sem.at[block]
            ),
            pltpu.make_async_copy(legendre_hbm.at[part], leg_buf.at[block], leg_sem.at[block]),
        )

    smalls = [
        pltpu.make_async_copy(source, target, small_sem.at[i])
        for i, (source, target) in enumerate(
            (
                (obs_hbm, obs_ref),
                (rows_hbm, rows_ref),
                (counts_hbm, counts_ref),
                (idx_hbm, idx_ref),
                (weight_hbm, weight_ref),
                (wave_hbm, wave_ref),
            )
        )
    ]
    for block in range(blocks):
        for one in load(block):
            one.start()
    for one in smalls:
        one.start()
    barrier = pltpu.get_barrier_semaphore()
    for step in range(1, nodes):
        pl.semaphore_signal(
            barrier, inc=1, device_id=where_is(peer(step)), device_id_type=pl.DeviceIdType.MESH
        )

    choose = selector(lat, items)
    @pl.loop(0, blocks)
    def _(block):
        for one in load(block):
            one.wait()
        product = dot(
            probe_buf[block].reshape(probe_local * field_count * 2 * SB, degrees),
            leg_buf[block].reshape(SB * lat, degrees),
            NT,
        )
        own = own_slot(lat)
        for p in range(probe_local):
            for w in range(waves):
                for e in range(fields):
                    for k in range(2):
                        first = (((p * waves + w) * fields + e) * 2 + k) * SB
                        item = (p * fields + e) * SB * lat
                        piece = jnp.where(own, product[first : first + SB], 0.0)
                        spread[w, k, block, :, item : item + SB * lat] = piece.astype(BF16)

    for w in range(waves):
        fourier = dot(choose, spread[w].reshape(2 * slots, items * SB * lat), NT).astype(BF16)
        for b in range(bands):
            send_1[b * waves + w] = fourier[b * rows : (b + 1) * rows]
    pl.semaphore_wait(barrier, nodes - 1)
    copies_1 = copies(send_1, recv_1, tx_1, rx_1)
    for one in copies_1:
        one.start()
    recv_1[me] = send_1[me]

    for one in smalls:
        one.wait()

    obs = jnp.concatenate([obs_ref[...]] * probe_local, axis=0)
    high = obs.astype(BF16).astype(F32)
    middle = (obs - high).astype(BF16).astype(F32)
    split = jnp.concatenate([high, middle, obs - high - middle], axis=0).astype(BF16)
    record = rows_ref[0]
    for node in range(nodes):
        pick = iota((obs.shape[1], capacity), 0) == record[node : node + 1, :]
        found = dot(split, jnp.where(pick, 1.0, 0.0).astype(BF16))
        send_w[node] = found[2 * items :] + found[items : 2 * items] + found[:items]
    copies_w = copies(send_w, recv_w, tx_w, rx_w)
    for one in copies_w:
        one.start()
    recv_w[me] = send_w[me]

    counts = counts_ref[...].astype(F32)
    mine = jnp.sum(jnp.where(iota(counts.shape, 1) == me, counts, 0.0), axis=1, keepdims=True)
    live = iota((nodes, capacity), 1).astype(F32) < mine
    for i in range(4):
        live_weight = jnp.where(live, weight_ref[i, 0], 0.0)
        for node in range(nodes):
            at = slice(node * capacity, (node + 1) * capacity)
            weights[i : i + 1, at] = live_weight[node : node + 1]
    for i in range(2):
        for node in range(nodes):
            at = slice(node * capacity, (node + 1) * capacity)
            point[i : i + 1, at] = idx_ref[i, 0, node : node + 1, :].astype(F32)

    factor = 1.0 / math.sqrt(total)
    for lane in range(0, total, 128):
        order = wave_ref[lane : lane + 128].reshape(1, 128).astype(F32)
        turn_c, turn_s = cos_sin(order * 128.0)

        @pl.loop(0, 2)
        def _(half):
            j = (iota((64, 128), 0) + half * 64).astype(F32)
            cos, sin = cos_sin(j * order)
            cos, sin = cos * factor, sin * factor
            for turn in range(NLON // 128):
                at = pl.ds(pl.multiple_of(half * 64, 64), 64)
                basis[turn, at, lane : lane + 128] = cos.astype(BF16)
                basis[turn, at, total + lane : total + lane + 128] = (-sin).astype(BF16)
                cos, sin = cos * turn_c - sin * turn_s, sin * turn_c + cos * turn_s

    row_of = jnp.floor((point[0:1, :] + 0.5) * (1.0 / NLON))
    west = point[0:1, :] - row_of * NLON
    east = point[1:2, :] - row_of * NLON
    west_weight, east_weight = [], []
    for l in range(lat_local):
        south, north = row_of == float(l), row_of == float(l - 1)
        west_weight.append(
            jnp.where(south, weights[0:1, :], jnp.where(north, weights[2:3, :], 0.0))
        )
        east_weight.append(
            jnp.where(south, weights[1:2, :], jnp.where(north, weights[3:4, :], 0.0))
        )

    @pl.loop(0, NLON // 64)
    def _(part):
        j = (iota((64, west.shape[1]), 0) + part * 64).astype(F32)
        at_west, at_east = j == west, j == east
        for l in range(lat_local):
            corner[l, part] = jnp.where(
                at_west, west_weight[l], jnp.where(at_east, east_weight[l], 0.0)
            ).astype(BF16)

    for one in copies_1:
        one.wait()
    for node in range(nodes):
        got = recv_1[node].astype(F32)
        for k in range(2):
            at = k * total + node * slots
            lanes[:, at : at + slots] = got[:, k * slots : (k + 1) * slots]
    table = basis[...].reshape(NLON, 2 * total)
    grid_values = dot(lanes[...].astype(BF16), table, NT)
    observed = jnp.zeros((2 * items, nodes * capacity), F32)
    for l in range(lat_local):
        here = grid_values[l * items : (l + 1) * items]
        both = jnp.concatenate([here, here - here.astype(BF16).astype(F32)], axis=0)
        observed += dot(both.astype(BF16), corner[l].reshape(NLON, nodes * capacity))
    observed = (observed[:items] + observed[items:]).astype(BF16).astype(F32)
    for one in copies_w:
        one.wait()
    for node in range(nodes):
        slot_w[:, node * capacity : (node + 1) * capacity] = recv_w[node]
    weighted = (slot_w[...] * observed).astype(BF16)
    adjoint = jnp.concatenate(
        [dot(weighted, corner[l].reshape(NLON, nodes * capacity), NT) for l in range(lat_local)],
        axis=0,
    ).astype(BF16)
    lanes[...] = dot(adjoint, table)
    for node in range(nodes):
        at = node * slots
        send_2[node] = jnp.concatenate(
            [lanes[:, at : at + slots], lanes[:, total + at : total + at + slots]], axis=1
        ).astype(BF16)
    copies_2 = copies(send_2, recv_2, tx_2, rx_2)
    for one in copies_2:
        one.start()
    recv_2[me] = send_2[me]
    for one in copies_2:
        one.wait()
    for b in range(bands):
        for w in range(waves):
            out_ref[w, b * rows : (b + 1) * rows, :] = recv_2[b * waves + w]


def synthesis_kernel(adjoint_ref, legendre_ref, out_ref, spread):
    probe_local, field_count, _, _, degrees = out_ref.shape
    waves = adjoint_ref.shape[0]
    fields = field_count // waves
    items = probe_local * fields
    lat = legendre_ref.shape[1]
    block = pl.program_id(0)

    @pl.when(block == 0)
    def _():
        choose = selector(lat, items)
        for w in range(waves):
            wide = dot(adjoint_ref[w], choose, TN)
            spread[w] = wide.astype(BF16).reshape(spread.shape[1:])

    own = jnp.where(own_slot(lat), 1.0, 0.0).astype(BF16)
    pieces = []
    for p in range(probe_local):
        for w in range(waves):
            for e in range(fields):
                for k in range(2):
                    item = (p * fields + e) * SB * lat
                    pieces.append(own * spread[w, k, block, :, item : item + SB * lat])
    result = dot(
        jnp.concatenate(pieces, axis=0), legendre_ref[...].reshape(SB * lat, degrees)
    )
    out_ref[...] = result.astype(BF16).reshape(out_ref.shape)


def fits_kernels(probes_spec, legendre, wave_order, obs_weight, send_rows, bands, waves):
    probe_local, field_count, _, slots, degrees = probes_spec.shape
    lat = legendre.shape[1]
    items = probe_local * field_count // waves
    return (
        slots % SB == 0
        and lat == 16
        and degrees % 128 == 0
        and wave_order.shape[0] % 128 == 0
        and field_count % waves == 0
        and obs_weight.shape[0] * probe_local == items
        and items == 8
        and lat % bands == 0
        and lat // bands * items % 16 == 0
        and 1 < bands * waves <= 8
        and bands * waves * send_rows.shape[2] % 128 == 0
        and obs_weight.shape[1] <= 1024
    )


def in_kernels(
    probes_spec, legendre, wave_order, obs_weight, send_rows, send_counts, interp_idx, interp_weight
):
    bands = lax.axis_size("band")
    waves = lax.axis_size("wave")
    nodes = bands * waves
    probe_local, field_count, _, slots, degrees = probes_spec.shape
    lat = legendre.shape[1]
    blocks = slots // SB
    items = probe_local * field_count // waves
    rows = lat // bands * items
    total = wave_order.shape[0]
    capacity = send_rows.shape[2]
    wide = items * SB * lat
    vmem = pl.BlockSpec(memory_space=pltpu.VMEM)
    hbm = pl.BlockSpec(memory_space=pltpu.HBM)
    dma = pltpu.SemaphoreType.DMA
    adjoint = pl.pallas_call(
        functools.partial(exchange_kernel, bands, waves),
        out_shape=jax.ShapeDtypeStruct((waves, bands * rows, 2 * slots), BF16),
        in_specs=[hbm] * 8,
        out_specs=vmem,
        scratch_shapes=[
            pltpu.VMEM(wave_order.shape, jnp.int32),
            pltpu.VMEM(obs_weight.shape, F32),
            pltpu.VMEM(send_rows.shape, jnp.int32),
            pltpu.VMEM(send_counts.shape, jnp.int32),
            pltpu.VMEM(interp_idx.shape, jnp.int32),
            pltpu.VMEM(interp_weight.shape, F32),
            pltpu.VMEM((blocks, probe_local, field_count, 2, SB, degrees), BF16),
            pltpu.VMEM((blocks, SB, lat, degrees), BF16),
            pltpu.VMEM((waves, 2, blocks, SB, wide), BF16),
            pltpu.VMEM((NLON // 128, 128, 2 * total), BF16),
            pltpu.VMEM((lat // bands, NLON // 64, 64, nodes * capacity), BF16),
            pltpu.VMEM((nodes, items, capacity), F32),
            pltpu.VMEM((nodes, items, capacity), F32),
            pltpu.VMEM((items, nodes * capacity), F32),
            pltpu.VMEM((nodes, rows, 2 * slots), BF16),
            pltpu.VMEM((nodes, rows, 2 * slots), BF16),
            pltpu.VMEM((nodes, rows, 2 * slots), BF16),
            pltpu.VMEM((nodes, rows, 2 * slots), BF16),
            pltpu.VMEM((rows, 2 * total), F32),
            pltpu.VMEM((8, nodes * capacity), F32),
            pltpu.VMEM((8, nodes * capacity), F32),
            dma((6,)),
            dma((blocks,)),
            dma((blocks,)),
            dma((nodes,)),
            dma((nodes,)),
            dma((nodes,)),
            dma((nodes,)),
            dma((nodes,)),
            dma((nodes,)),
        ],
        compiler_params=pltpu.CompilerParams(
            collective_id=0, has_side_effects=True, vmem_limit_bytes=40 * 2**20
        ),
    )(
        *(
            pltpu.with_memory_space_constraint(one, pltpu.HBM)
            for one in (
                probes_spec, legendre, wave_order, obs_weight, send_rows, send_counts, interp_idx,
                interp_weight,
            )
        )
    )
    return pl.pallas_call(
        synthesis_kernel,
        grid=(blocks,),
        out_shape=jax.ShapeDtypeStruct(probes_spec.shape, BF16),
        in_specs=[
            pl.BlockSpec(adjoint.shape, lambda i: (0, 0, 0)),
            pl.BlockSpec((SB, lat, degrees), lambda i: (i, 0, 0)),
        ],
        out_specs=pl.BlockSpec(
            (probe_local, field_count, 2, SB, degrees), lambda i: (0, 0, 0, i, 0)
        ),
        scratch_shapes=[pltpu.VMEM((waves, 2, blocks, SB, wide), BF16)],
        compiler_params=pltpu.CompilerParams(vmem_limit_bytes=40 * 2**20),
    )(adjoint, legendre)


def make_basis(wave_numbers, lon_count, wave_total):
    columns = jnp.arange(lon_count, dtype=jnp.int32)
    phases = wave_numbers[:, None] * columns[None, :] % lon_count
    angles = phases.astype(jnp.float32) * (2.0 * math.pi / lon_count)
    factor = 1.0 / math.sqrt(wave_total)
    return jnp.stack([factor * jnp.cos(angles), -factor * jnp.sin(angles)]).astype(jnp.bfloat16)


def in_general(
    probes_spec, legendre, wave_order, obs_weight, send_rows, send_counts, interp_idx, interp_weight
):
    band_count = lax.axis_size("band")
    wave_count = lax.axis_size("wave")
    node_count = band_count * wave_count
    probe_local, field_count, _, slot_local, degree_count = probes_spec.shape
    field_local = field_count // wave_count
    lat_local = legendre.shape[1] // band_count
    wave_total = wave_order.shape[0]
    capacity = send_rows.shape[2]
    points = lat_local * NLON
    spec_split = probes_spec.reshape(
        probe_local, wave_count, field_local, 2, slot_local, degree_count
    )
    legendre_split = legendre.reshape(slot_local, band_count, lat_local, degree_count)
    fourier = jnp.einsum(
        "pwgksn,sbln->bwpglks", spec_split, legendre_split, preferred_element_type=jnp.float32
    ).astype(jnp.bfloat16)
    fourier_basis = make_basis(wave_order, NLON, wave_total)
    flat_fourier = fourier.reshape(node_count, probe_local, field_local, lat_local, 2, slot_local)
    grid_values = jnp.einsum(
        "pglks,ksj->pglj",
        lax.all_to_all(flat_fourier, ("band", "wave"), split_axis=0, concat_axis=5, tiled=True)[0],
        fourier_basis,
        preferred_element_type=jnp.float32,
    )
    grid_flat = grid_values.reshape(probe_local, field_local, points)
    node_index = lax.axis_index(("band", "wave"))
    counts_here = lax.dynamic_slice_in_dim(send_counts, node_index, 1, 1)[:, 0]
    live_mask = jnp.arange(capacity, dtype=jnp.int32)[None, :] < counts_here[:, None]
    corner_index = interp_idx[:, 0].reshape(-1)
    corner_weight = interp_weight[:, 0]
    values = jnp.take(grid_flat, corner_index, axis=2).reshape(
        probe_local, field_local, 4, node_count, capacity
    )
    corner_sums = jnp.sum(values * corner_weight[None, None], axis=2)
    observed = jnp.where(live_mask[None, None], corner_sums, 0.0).astype(jnp.bfloat16)
    record_index = send_rows[0].reshape(-1)
    slot_weight = jnp.take(obs_weight, record_index, axis=1).reshape(
        field_local, node_count, capacity
    )
    scaled = (
        slot_weight[None]
        * lax.all_to_all(
            observed, ("band", "wave"), split_axis=2, concat_axis=2, tiled=True
        ).astype(jnp.float32)
    ).astype(jnp.bfloat16)
    weighted = lax.all_to_all(scaled, ("band", "wave"), split_axis=2, concat_axis=2, tiled=True)
    scattered = (corner_weight[None, None] * weighted.astype(jnp.float32)[:, :, None]).reshape(
        probe_local, field_local, -1
    )
    adjoint = (
        jnp.zeros((probe_local, field_local, points), jnp.float32)
        .at[:, :, corner_index]
        .add(scattered)
    )
    adjoint = adjoint.reshape(probe_local, field_local, lat_local, NLON).astype(jnp.bfloat16)
    fourier_adjoint = jnp.einsum(
        "pglj,ksj->pglks", adjoint, fourier_basis, preferred_element_type=jnp.float32
    ).astype(jnp.bfloat16)
    split_adjoint = fourier_adjoint.reshape(
        probe_local, field_local, lat_local, 2, node_count, slot_local
    )
    received = lax.all_to_all(
        split_adjoint, ("band", "wave"), split_axis=4, concat_axis=4, tiled=True
    )
    item_count = received.shape[0]
    parted = received.reshape(
        item_count, field_local, lat_local, 2, band_count, wave_count, slot_local
    )
    result = jnp.einsum(
        "pglkbws,sbln->pwgksn", parted, legendre_split, preferred_element_type=jnp.float32
    )
    return result.reshape(item_count, field_count, 2, slot_local, degree_count).astype(jnp.bfloat16)


def on_device(probes_spec, legendre, wave_order, obs_weight, send_rows, *others):
    sizes = lax.axis_size("band"), lax.axis_size("wave")
    fits = fits_kernels(probes_spec, legendre, wave_order, obs_weight, send_rows, *sizes)
    run = in_kernels if fits else in_general
    return run(probes_spec, legendre, wave_order, obs_weight, send_rows, *others)


def solution(mesh):
    placed = (
        P(("groups", "probe"), None, None, ("band", "wave"), None),
        P(("band", "wave"), None, None),
        P(),
        P(None, ("groups", "band", "wave")),
        P(("groups", "band", "wave"), None, None),
        P("groups", None),
        P(None, ("groups", "band", "wave"), None, None),
        P(None, ("groups", "band", "wave"), None, None),
    )
    return jax.shard_map(
        on_device,
        mesh=mesh,
        in_specs=placed,
        out_specs=P(("groups", "probe"), None, None, ("band", "wave"), None),
        check_vma=False,
    )
```
